32 devices in a mesh: expert: 8 (over y, x, core), narrow: 4 (over z).
Axes of the slice: x: 2, y: 2, z: 4, core: 2. Of those that a mesh axis runs over, the one named last changes fastest.
Arguments:
- feats: bfloat16 [32768, 512], P(('expert', 'narrow')), may hold values from -6 to 6
- cotangent: bfloat16 [32768, 512], P(('expert', 'narrow')), may hold values from -0.59765625 to 0.59765625
- routes: int32 [32768, 1], P(('expert', 'narrow')), may hold values from 0 to 7; in each aligned block of 1024 rows (0 to 1023, 1024 to 2047, ...) at most 256 rows name the same one
- image_ids: int32 [32768], P(('expert', 'narrow')), may hold values from 0 to 255, as said below
- codes: bfloat16 [256, 48], replicated, may hold values from -6 to 6
- params: bfloat16 [8, 2096, 512], P('expert', 'narrow'), may hold values from -0.375 to 0.375
Outputs:
- out_rows: bfloat16 [32768, 512], P(('expert', 'narrow'))
- feat_grad: bfloat16 [32768, 512], P(('expert', 'narrow'))
- param_grad: float32 [8, 2096, 512], P('expert', 'narrow')
- code_grad: float32 [256, 48], P(('expert', 'narrow'))
The draws below stay inside these ranges and needn't reach their ends.
Inputs may be any that keep to these rules, and one draw needn't show every extreme that they name: `routes`: among the rows of one device no expert is named more than 256 times, and on some device some expert is named exactly 256 times. `image_ids`: the rows of the device with flat index f over expert+narrow (expert index slowest) name only images f * 8 to f * 8 + 2 * 8 - 1, taken modulo 256.
All inputs are finite; a program needn't handle non-finite values.
Results may differ from the reference program's by a relative error of at most 0.017.
Values may be sent and summed in bfloat16 or wider, within the bound.
A program may use at most 128 MiB of HBM per device.

```python
import math
import jax
import jax.numpy as jnp
import numpy as np
from jax import lax

D = 512
CODE = 48
LAYERS = 4
ROWS_DEV = 1024
IMG_DEV = 8
EXPERTS = 8
CAP = 256
PROWS = 2096
ROWS = 32768
IMAGES = 256
N_EXPERT = 8
N_NARROW = 4


def draw_image_ids(key, part):
    row_numbers = jnp.arange(ROWS, dtype=jnp.int32)
    device_no = row_numbers // ROWS_DEV
    jitter = jax.random.randint(key, (ROWS,), 0, 2 * IMG_DEV, dtype=jnp.int32)
    return (device_no * IMG_DEV + jitter) % IMAGES


def block_scale(stream_key, extent, shards, low, top_value):
    gain, own = 1.0, jax.random.fold_in(stream_key, 6)
    for dim, blocks in shards:
        heights = jnp.exp(jax.random.uniform(jax.random.fold_in(own, dim), (blocks,), jnp.float32, low / len(shards), top_value / len(shards)))
        gain = gain * jnp.repeat(heights, extent[dim] // blocks).reshape([-1 if axis == dim else 1 for axis in range(len(extent))])
    return gain


def assign_block(own_key, own, number, rows, number_of, top, most, lean):
    ranking = jax.random.permutation(own_key, number_of)
    crowded, common = portions_of(number_of, rows * top, most, lean, True), portions_of(number_of, rows * top, most, lean, False)
    places = jnp.arange(number_of)

    def named(sizes, offset_by):
        used = int((sizes > 0).sum())
        fixed = max(1, used // 4)
        shifted = fixed + (places - fixed + offset_by * (used - fixed)) % max(1, number_of - fixed)
        return jnp.zeros((number_of,), jnp.int32).at[ranking[jnp.where(places < fixed, places, shifted)]].set(jnp.asarray(sizes, jnp.int32))

    sizes = jnp.where(number % 4 == 0, named(crowded, number // 4), named(common, number - number // 4 - 1))
    mixed = jax.random.permutation(jax.random.fold_in(own, 3), number_of)
    source_of, receiver = mixed[0:number_of // 2 * 2:2], mixed[1:number_of // 2 * 2:2]
    slack = jnp.minimum(sizes[source_of] - 1, most - sizes[receiver]) // 2
    slack = jnp.where((source_of == ranking[0]) | (receiver == ranking[0]) | (sizes[receiver] == 0), 0, jnp.maximum(slack, 0))
    shifted = jax.random.randint(jax.random.fold_in(own, 4), (number_of // 2,), 0, 1 << 20) % (slack + 1)
    sizes = sizes.at[source_of].add(-shifted).at[receiver].add(shifted)
    members = jnp.searchsorted(jnp.cumsum(sizes), jnp.arange(rows * top), side="right").astype(jnp.int32)
    table = members.reshape(top, rows).T
    table = table[jax.random.permutation(jax.random.fold_in(own, 1), rows)]
    offset_by = jax.random.randint(jax.random.fold_in(own, 2), (rows, 1), 0, top)
    return jnp.take_along_axis(table, (jnp.arange(top)[None, :] + offset_by) % top, axis=1)


def portions_of(count, total, most, slope, full):
    loads = [(1 << 20) // math.isqrt(standing ** slope) + 1 for standing in range(1, count + 1)]
    largest = most if full else min(most, max(-(-total // count), total * loads[0] // sum(loads)))
    least = 1 if total - largest >= count - 1 else 0
    given, spare = [largest] + [least] * (count - 1), total - largest - least * (count - 1)
    while spare > 0:
        movable = [i for i in range(1, count) if given[i] < largest] or [i for i in range(1, count) if given[i] < most]
        whole, left = sum([loads[i] for i in movable]), spare
        for i in movable:
            addition = min(most - given[i], max(1, left * loads[i] // whole), spare)
            given[i] = given[i] + addition
            spare = spare - addition
    return np.array(given)


def scatter_about(own_key, dims, deviation, bound, cuts=(), held_as=jnp.bfloat16):
    factor_of = block_scale(own_key, dims, cuts, -0.22, 0.18) if cuts else 1.0
    entries = jax.random.normal(own_key, dims, jnp.float32) * deviation * factor_of
    return jnp.minimum(jnp.maximum(entries, -bound), bound).astype(held_as)


def setup_inputs(seed: int = 0) -> dict:
    arg_keys = jax.random.split(jax.random.key(seed), 7)
    feats = scatter_about(arg_keys[0], (ROWS, D), 1.0, 6.0, ((0, 32),))
    cotangent = scatter_about(arg_keys[1], (ROWS, D), 0.1, 0.59765625, ((0, 32),))
    routes_keys = jax.random.split(jax.random.fold_in(arg_keys[2], 1), ROWS // ROWS_DEV)
    routes_turns = jax.random.permutation(jax.random.fold_in(arg_keys[2], 3), ROWS // ROWS_DEV)
    routes = jax.vmap(lambda own, number: assign_block(jax.random.fold_in(arg_keys[2], 2), own, number, ROWS_DEV, EXPERTS, 1, CAP, 2))(routes_keys, routes_turns).reshape((ROWS, 1))
    image_ids = draw_image_ids(jax.random.fold_in(arg_keys[6], 71), 0)
    codes = scatter_about(arg_keys[4], (IMAGES, CODE), 1.0, 6.0)
    params = scatter_about(arg_keys[5], (EXPERTS, PROWS, D), (D // 2) ** -0.5, 0.375, ((0, 8), (1, 4)))
    return {"feats": feats, "cotangent": cotangent, "routes": routes, "image_ids": image_ids, "codes": codes, "params": params}


def forward(weights, row_block, code_rows, depth_count):
    feature_width = row_block.shape[1]
    code_matrix = weights[depth_count * feature_width:]
    current = row_block
    inputs = []
    preacts = []
    for layer_no in range(depth_count):
        inputs.append(current)
        layer_weights = weights[layer_no * feature_width:(layer_no + 1) * feature_width]
        preact = jnp.dot(current, layer_weights, preferred_element_type=jnp.float32)
        if layer_no == 0:
            preact = preact + jnp.dot(code_rows, code_matrix, preferred_element_type=jnp.float32)
        preacts.append(preact)
        current = jax.nn.silu(preact).astype(jnp.bfloat16)
    inputs.append(code_rows)
    return current, tuple(inputs), tuple(preacts)


def backward(weights, preacts, cotangent, depth_count):
    feature_width = cotangent.shape[1]
    code_matrix = weights[depth_count * feature_width:]
    upstream = cotangent.astype(jnp.float32)
    errors = []
    for layer_no in range(depth_count - 1, -1, -1):
        preact = preacts[layer_no]
        sigmoid_value = jax.nn.sigmoid(preact)
        error_rows = (upstream * sigmoid_value * (1.0 + preact * (1.0 - sigmoid_value))).astype(jnp.bfloat16)
        errors.insert(0, error_rows)
        layer_weights = weights[layer_no * feature_width:(layer_no + 1) * feature_width]
        upstream = jnp.dot(error_rows, layer_weights.T, preferred_element_type=jnp.float32)
    code_back = jnp.dot(errors[0], code_matrix.T, preferred_element_type=jnp.float32).astype(jnp.bfloat16)
    return upstream.astype(jnp.bfloat16), code_back, tuple(errors)


def param_terms(inputs, errors):
    depth_count = len(errors)
    blocks = []
    for layer_no in range(depth_count):
        blocks.append(jnp.dot(inputs[layer_no].T, errors[layer_no], preferred_element_type=jnp.float32))
    blocks.append(jnp.dot(inputs[depth_count].T, errors[0], preferred_element_type=jnp.float32))
    return jnp.concatenate(blocks, axis=0)


def reference(feats, cotangent, routes, image_ids, codes, params):
    devices = N_EXPERT * N_NARROW
    experts = params.shape[0]
    targets = routes[:, 0].reshape(devices, ROWS_DEV)
    onehot = (targets[:, :, None] == jnp.arange(experts, dtype=jnp.int32)[None, None, :]).astype(jnp.int32)
    slot_ids = jnp.sum(jnp.cumsum(onehot, axis=1) * onehot, axis=2) - 1
    positions = jnp.arange(devices, dtype=jnp.int32)[:, None] * CAP + slot_ids
    row_numbers = jnp.arange(ROWS, dtype=jnp.int32).reshape(devices, ROWS_DEV)
    slot_table = jnp.full((experts, devices * CAP), ROWS, jnp.int32).at[targets, positions].set(row_numbers)
    code_rows = codes[image_ids]

    def per_expert(state_now, pieces):
        out_all, feat_all, code_all = state_now
        weights, picked = pieces
        safe_ids = jnp.minimum(picked, ROWS - 1)
        live_mask = (picked < ROWS)[:, None]
        chosen_rows = jnp.where(live_mask, feats[safe_ids], jnp.zeros_like(feats[safe_ids]))
        chosen_codes = jnp.where(live_mask, code_rows[safe_ids], jnp.zeros_like(code_rows[safe_ids]))
        chosen_cot = jnp.where(live_mask, cotangent[safe_ids], jnp.zeros_like(cotangent[safe_ids]))
        outcome, inputs, preacts = forward(weights, chosen_rows, chosen_codes, LAYERS)
        feat_back, code_back, errors = backward(weights, preacts, chosen_cot, LAYERS)
        grad_terms = param_terms(inputs, errors)
        out_all = out_all.at[picked].set(outcome, mode="drop")
        feat_all = feat_all.at[picked].set(feat_back, mode="drop")
        code_all = code_all.at[picked].set(code_back, mode="drop")
        return (out_all, feat_all, code_all), grad_terms

    initial = (jnp.zeros((ROWS, D), jnp.bfloat16), jnp.zeros((ROWS, D), jnp.bfloat16), jnp.zeros((ROWS, CODE), jnp.bfloat16))
    finals, param_grad = lax.scan(per_expert, initial, (params, slot_table))
    out_rows, feat_grad, code_row_grad = finals
    code_grad = jax.ops.segment_sum(code_row_grad.astype(jnp.float32), image_ids, num_segments=IMAGES)
    return out_rows, feat_grad, param_grad, code_grad
```

```python
import functools

import jax
import jax.numpy as jnp
from jax import lax
from jax.experimental import pallas as pl
from jax.experimental.pallas import tpu as pltpu
from jax.sharding import PartitionSpec as P

LAYERS = 4
IMG_DEV = 8
GROUP = 256
LANES = 128
F32 = jnp.float32
BF16 = jnp.bfloat16


def xor(a, b, extent):
    total, bit = 0, 1
    while bit < extent:
        x = lax.rem(lax.div(a, bit), 2)
        y = lax.rem(lax.div(b, bit), 2)
        total = total + bit * (x + y - 2 * x * y)
        bit *= 2
    return total


def mm(a, b):
    return jnp.dot(a, b, preferred_element_type=F32)


def mm_nt(a, b):
    return lax.dot_general(a, b, (((1,), (1,)), ((), ())), preferred_element_type=F32)


def mm_tn(a, b):
    return lax.dot_general(a, b, (((0,), (0,)), ((), ())), preferred_element_type=F32)


def kernel(
    E, N, IMAGES, feats, cot, tgt_row, tgt_col, ids_row, codes, params,
    out_rows, feat_grad, param_grad, code_grad,
    send_a, send_b, send_i, send_w, send_d,
    recv_a, recv_b, recv_i, recv_w, recv_d, recv_o, recv_f,
    shards, wide, weights, code_w, acts, slopes, code_rows, pick, unpick, oh_col,
    half, half_in, sems, zsems, nsems,
):
    rows, width = feats.shape
    prows = param_grad.shape[0]
    cap = 2 * rows // E
    per = GROUP // cap
    groups = 2 * rows // GROUP
    me = lax.axis_index("expert")
    z = lax.axis_index("narrow")
    flat = me * N + z
    following = lax.rem(flat + 1, E * N)
    preceding = lax.rem(flat + E * N - 1, E * N)

    def peer(k):
        return {"expert": xor(me, k, E)}

    def at_flat(f):
        return {"expert": lax.div(f, N), "narrow": lax.rem(f, N)}

    barrier = pltpu.get_barrier_semaphore()
    for k in range(1, E):
        pl.semaphore_signal(barrier, inc=1, device_id=peer(k))
    for j in range(1, N):
        pl.semaphore_signal(barrier, inc=1, device_id={"narrow": lax.rem(z + j, N)})
    pl.semaphore_signal(barrier, inc=1, device_id=at_flat(following))
    pl.semaphore_signal(barrier, inc=1, device_id=at_flat(preceding))
    pl.semaphore_wait(barrier, E - 1 + N - 1 + 2)

    def chunk(ref, k):
        return ref.at[pl.ds(pl.multiple_of(k * cap, cap), cap)]

    def exchange(which, src, dst, k):
        return pltpu.make_async_remote_copy(
            src_ref=src, dst_ref=dst, send_sem=sems.at[which, 0, k],
            recv_sem=sems.at[which, 1, k], device_id=peer(k))

    def copy_a(k):
        return exchange(0, chunk(send_a, k), chunk(recv_a, k), k)

    def copy_b(k):
        return exchange(1, chunk(send_b, k), chunk(recv_b, k), k)

    def copy_o(k):
        return exchange(2, chunk(send_a, k), chunk(recv_o, k), k)

    def copy_f(k):
        return exchange(3, chunk(send_b, k), chunk(recv_f, k), k)

    def copy_i(k):
        return exchange(4, send_i.at[lax.div(k, per)], recv_i.at[k], k)

    def copy_w(k):
        return exchange(5, send_w.at[k], recv_w.at[k], k)

    def each_peer(g, act):
        for i in range(per):
            k = g * per + i

            @pl.when(k != 0)
            def _():
                act(k)

    def line(way, shard):
        return pltpu.make_async_remote_copy(
            src_ref=shards.at[shard], dst_ref=shards.at[shard],
            send_sem=zsems.at[way, 0, shard], recv_sem=zsems.at[way, 1, shard],
            device_id={"narrow": z + 1 - 2 * way})

    def relay(step, begin):
        up, down = z - step, z + step

        @pl.when((up >= 0) & (z + 1 < N))
        def _():
            begin(line(0, up))

        @pl.when((down < N) & (z > 0))
        def _():
            begin(line(1, down))

    shards[z] = params[...]
    relay(0, lambda copy: copy.start())

    number = lax.broadcasted_iota(jnp.int32, (E, rows), 0)
    partner = jnp.bitwise_xor(tgt_row[...], me)
    named = jnp.where(jnp.broadcast_to(partner, (E, rows)) == number, 1.0, 0.0)
    upper = jnp.where(
        lax.broadcasted_iota(jnp.int32, (rows, rows), 0)
        <= lax.broadcasted_iota(jnp.int32, (rows, rows), 1), 1.0, 0.0).astype(BF16)
    count = mm(named.astype(BF16), upper)
    slot = jnp.sum(named * count, axis=0, keepdims=True) - 1.0
    place = (partner * cap).astype(F32) + slot
    offset = ids_row[...] - flat * IMG_DEV
    offset = jnp.where(offset < 0, offset + IMAGES, offset) + 1
    offset8 = jnp.broadcast_to(offset.astype(F32), (8, rows)).astype(BF16)

    def pack_feats(i, carry):
        g = groups - 1 - i
        span = pl.ds(pl.multiple_of(g * GROUP, GROUP), GROUP)
        wanted = (lax.broadcasted_iota(jnp.int32, (GROUP, rows), 0) + g * GROUP).astype(F32)
        chosen = jnp.where(jnp.broadcast_to(place, (GROUP, rows)) == wanted, 1.0, 0.0).astype(BF16)
        pick[span, :] = chosen
        send_a[span, :] = mm(chosen, feats[...]).astype(BF16)
        send_i[g] = mm_nt(offset8, chosen)
        each_peer(g, lambda k: (copy_a(k).start(), copy_i(k).start()))
        return carry

    lax.fori_loop(0, groups, pack_feats, 0)
    recv_a[:cap, :] = send_a[:cap, :]
    recv_i[0] = send_i[0]

    def pack_cot(i, carry):
        g = groups - 1 - i
        span = pl.ds(pl.multiple_of(g * GROUP, GROUP), GROUP)
        send_b[span, :] = mm(pick[span, :], cot[...]).astype(BF16)
        each_peer(g, lambda k: copy_b(k).start())
        return carry

    lax.fori_loop(0, groups, pack_cot, 0)
    recv_b[:cap, :] = send_b[:cap, :]

    lane = lax.broadcasted_iota(jnp.int32, (rows, LANES), 1)
    partner_col = jnp.bitwise_xor(tgt_col[...], me)
    oh_col[...] = jnp.where(
        jnp.broadcast_to(partner_col, (rows, LANES)) == lane, 1.0, 0.0).astype(BF16)

    def unpick_tile(i, carry):
        span = pl.ds(pl.multiple_of(i * GROUP, GROUP), GROUP)
        lower = jnp.where(
            lax.broadcasted_iota(jnp.int32, (GROUP, rows), 1)
            <= lax.broadcasted_iota(jnp.int32, (GROUP, rows), 0) + i * GROUP, 1.0, 0.0).astype(BF16)
        mine = oh_col[span, :].astype(F32)
        seen = mm(lower, oh_col[...])
        base = (lax.broadcasted_iota(jnp.int32, (GROUP, LANES), 1) * cap - 1).astype(F32)
        where = jnp.sum(mine * (seen + base), axis=1, keepdims=True)
        index = lax.broadcasted_iota(jnp.int32, (GROUP, 2 * rows), 1).astype(F32)
        unpick[span, :] = jnp.where(
            jnp.broadcast_to(where, (GROUP, 2 * rows)) == index, 1.0, 0.0).astype(BF16)
        return carry

    for step in range(1, N):
        if step == 1:
            lax.fori_loop(0, rows // GROUP, unpick_tile, 0)

        @pl.when(z - step >= 0)
        def _():
            line(0, z - step).wait_recv()

        @pl.when(z + step < N)
        def _():
            line(1, z + step).wait_recv()

        if step < N - 1:
            relay(step, lambda copy: copy.start())

    depth = LAYERS * width
    for n in range(N):
        wide[n * prows : (n + 1) * prows, :] = shards[n].astype(F32)[:prows]
    weights[...] = wide[:depth, :].astype(BF16)
    code_w[...] = jnp.zeros_like(code_w)
    code_w[: N * prows - depth, :] = wide[depth : N * prows, :].astype(BF16)

    def picked_images(g, i):
        held = recv_i[g * per + i][0:1, :]
        image = (lax.broadcasted_iota(jnp.int32, (16, GROUP), 0) + 1).astype(F32)
        hit = jnp.broadcast_to(held, (16, GROUP)) == image
        if per > 1:
            inside = lax.div(lax.broadcasted_iota(jnp.int32, (16, GROUP), 1), cap) == i
            hit = hit & inside
        return jnp.where(hit, 1.0, 0.0).astype(BF16)

    def onward(t, carry):
        g = groups - 1 - t
        span = pl.ds(pl.multiple_of(g * GROUP, GROUP), GROUP)
        each_peer(g, lambda k: (copy_a(k).wait_recv(), copy_i(k).wait_recv()))
        looked = jnp.zeros((GROUP, LANES), F32)
        for i in range(per):
            source = xor(me, g * per + i, E) * N + z
            first = pl.multiple_of(source * IMG_DEV, IMG_DEV)
            looked = looked + mm_tn(picked_images(g, i), codes[pl.ds(first, 16), :].astype(BF16))
        looked = looked.astype(BF16)
        code_rows[span, :] = looked
        current = recv_a[span, :]
        for l in range(LAYERS):
            pre = mm(current, weights[l * width : (l + 1) * width, :])
            if l == 0:
                pre = pre + mm(looked, code_w[...])
            s = 1.0 / (1.0 + jnp.exp(-pre))
            current = (pre * s).astype(BF16)
            slopes[l, span, :] = (s * (1.0 + pre * (1.0 - s))).astype(BF16)
            if l < LAYERS - 1:
                acts[l, span, :] = current
        each_peer(g, lambda k: copy_a(k).wait_send())
        send_a[span, :] = current
        each_peer(g, lambda k: copy_o(k).start())
        return carry

    lax.fori_loop(0, groups, onward, 0)
    recv_o[:cap, :] = send_a[:cap, :]

    wide[...] = jnp.zeros_like(wide)

    def back(t, carry):
        g = groups - 1 - t
        span = pl.ds(pl.multiple_of(g * GROUP, GROUP), GROUP)
        each_peer(g, lambda k: (copy_b(k).wait_recv(), copy_b(k).wait_send()))
        up = recv_b[span, :].astype(F32)
        for l in range(LAYERS - 1, -1, -1):
            err = (up * slopes[l, span, :].astype(F32)).astype(BF16)
            slopes[l, span, :] = err
            up = mm_nt(err, weights[l * width : (l + 1) * width, :])
        send_b[span, :] = up.astype(BF16)
        each_peer(g, lambda k: copy_f(k).start())
        code_back = mm_nt(err, code_w[...]).astype(BF16)
        for i in range(per):
            send_w[g * per + i] = mm(picked_images(g, i), code_back)
        each_peer(g, lambda k: copy_w(k).start())
        for l in range(LAYERS):
            values = recv_a[span, :] if l == 0 else acts[l - 1, span, :]
            wide[l * width : (l + 1) * width, :] += mm_tn(values, slopes[l, span, :])
        wide[depth:, :] += mm_tn(code_rows[span, :], err)
        return carry

    lax.fori_loop(0, groups, back, 0)
    recv_f[:cap, :] = send_b[:cap, :]
    recv_w[0] = send_w[0]

    padded = shards.shape[1]
    for n in range(N):
        send_d[n] = wide[n * prows : n * prows + padded, :].astype(BF16)

    def copy_d(j):
        dest = lax.rem(z + j, N)
        return pltpu.make_async_remote_copy(
            src_ref=send_d.at[dest], dst_ref=recv_d.at[j], send_sem=zsems.at[2, 0, j],
            recv_sem=zsems.at[2, 1, j], device_id={"narrow": dest})

    for j in range(1, N):
        copy_d(j).start()

    each = recv_w[0]
    for k in range(1, E):
        copy_w(k).wait_recv()
        each = each + recv_w[k]
    half[...] = each[IMG_DEV:]
    pass_on = pltpu.make_async_remote_copy(
        src_ref=half, dst_ref=half_in, send_sem=nsems.at[0], recv_sem=nsems.at[1],
        device_id=at_flat(following))
    pass_on.start()

    for copy, held, result in ((copy_o, recv_o, out_rows), (copy_f, recv_f, feat_grad)):
        for k in range(1, E):
            copy(k).wait_recv()

        def unpack(i, carry, held=held, result=result):
            span = pl.ds(pl.multiple_of(i * GROUP, GROUP), GROUP)
            result[span, :] = mm(unpick[span, :], held[...]).astype(BF16)
            return carry

        lax.fori_loop(0, rows // GROUP, unpack, 0)

    pass_on.wait()
    code_grad[...] = each[:IMG_DEV] + half_in[...]

    for j in range(1, N):
        copy_d(j).wait_recv()
    total = send_d[z].astype(F32)
    for j in range(1, N):
        total = total + recv_d[j].astype(F32)
    param_grad[...] = total[:prows]

    for step in range(N - 1):
        relay(step, lambda copy: copy.wait_send())
    for j in range(1, N):
        copy_d(j).wait_send()
    for k in range(1, E):
        for copy in (copy_o, copy_f, copy_i, copy_w):
            copy(k).wait_send()


def body(E, N, feats, cotangent, routes, image_ids, codes, params):
    rows, width = feats.shape
    prows = params.shape[1]
    padded = -(-prows // 16) * 16
    images, code = codes.shape
    deep = LAYERS * width + LANES
    around = jnp.concatenate([codes, codes[:IMG_DEV]], axis=0).astype(F32)
    around = jnp.pad(around, ((0, 0), (0, LANES - code)))
    shard = jnp.pad(params[0], ((0, padded - prows), (0, 0)))
    vm = pl.BlockSpec(memory_space=pltpu.VMEM)
    slots = 2 * rows
    buffer = pltpu.VMEM((slots, width), BF16)
    per = GROUP // (slots // E)
    groups = slots // GROUP
    out_rows, feat_grad, param_grad, code_grad = pl.pallas_call(
        functools.partial(kernel, E, N, images),
        out_shape=[
            jax.ShapeDtypeStruct((rows, width), BF16),
            jax.ShapeDtypeStruct((rows, width), BF16),
            jax.ShapeDtypeStruct((prows, width), F32),
            jax.ShapeDtypeStruct((IMG_DEV, LANES), F32),
        ],
        in_specs=[vm] * 7,
        out_specs=[vm] * 4,
        scratch_shapes=[
            buffer, buffer,
            pltpu.VMEM((groups, 8, GROUP), F32),
            pltpu.VMEM((E, 16, LANES), F32),
            pltpu.VMEM((N, padded, width), BF16),
            buffer, buffer,
            pltpu.VMEM((E, 8, GROUP), F32),
            pltpu.VMEM((E, 16, LANES), F32),
            pltpu.VMEM((N, padded, width), BF16),
            buffer, buffer,
            pltpu.VMEM((N, padded, width), BF16),
            pltpu.VMEM((deep, width), F32),
            pltpu.VMEM((LAYERS * width, width), BF16),
            pltpu.VMEM((LANES, width), BF16),
            pltpu.VMEM((LAYERS - 1, slots, width), BF16),
            pltpu.VMEM((LAYERS, slots, width), BF16),
            pltpu.VMEM((slots, LANES), BF16),
            pltpu.VMEM((slots, rows), BF16),
            pltpu.VMEM((rows, slots), BF16),
            pltpu.VMEM((rows, LANES), BF16),
            pltpu.VMEM((IMG_DEV, LANES), F32),
            pltpu.VMEM((IMG_DEV, LANES), F32),
            pltpu.SemaphoreType.DMA((6, 2, E)),
            pltpu.SemaphoreType.DMA((3, 2, N)),
            pltpu.SemaphoreType.DMA((2,)),
        ],
        compiler_params=pltpu.CompilerParams(
            collective_id=0, has_side_effects=True, vmem_limit_bytes=60 * 1024 * 1024),
    )(
        feats, cotangent, routes.reshape(1, rows), routes,
        image_ids.reshape(1, rows), around, shard,
    )
    return out_rows, feat_grad, param_grad[None], code_grad[:, :code]


def solution(mesh):
    E, N = mesh.shape["expert"], mesh.shape["narrow"]
    rows = P(("expert", "narrow"), None)
    held = P("expert", "narrow", None)
    return jax.shard_map(
        functools.partial(body, E, N), mesh=mesh,
        in_specs=(rows, rows, rows, P(("expert", "narrow")), P(), held),
        out_specs=(rows, rows, held, rows), check_vma=False)
```

```python
import functools

import jax
import jax.numpy as jnp
from jax import lax
from jax.experimental import pallas as pl
from jax.experimental.pallas import tpu as pltpu
from jax.sharding import PartitionSpec as P

LAYERS = 4
IMG_DEV = 8
GROUP = 256
LANES = 128
F32 = jnp.float32
BF16 = jnp.bfloat16


def xor(a, b, extent):
    total, bit = 0, 1
    while bit < extent:
        x = lax.rem(lax.div(a, bit), 2)
        y = lax.rem(lax.div(b, bit), 2)
        total = total + bit * (x + y - 2 * x * y)
        bit *= 2
    return total


def mm(a, b):
    return jnp.dot(a, b, preferred_element_type=F32)


def mm_nt(a, b):
    return lax.dot_general(a, b, (((1,), (1,)), ((), ())), preferred_element_type=F32)


def mm_tn(a, b):
    return lax.dot_general(a, b, (((0,), (0,)), ((), ())), preferred_element_type=F32)


def kernel(
    E, N, IMAGES, feats, cot, tgt_row, ids_row, codes_t, params,
    out_rows, feat_grad, param_grad, code_grad,
    send_a, send_b, send_i, send_w, send_d,
    recv_a, recv_b, recv_i, recv_w, recv_d, recv_o, recv_f,
    shards, wide, weights, code_w, acts, slopes, code_rows, pick, place_col,
    ups, codes, send_c, recv_c, half, half_in, sems, zsems, nsems,
):
    rows, width = feats.shape
    prows = params.shape[1]
    cap = 2 * rows // E
    per = GROUP // cap
    groups = 2 * rows // GROUP
    padded = shards.shape[1]
    depth = LAYERS * width
    extra = N * prows - depth
    me = lax.axis_index("expert")
    z = lax.axis_index("narrow")
    flat = me * N + z
    following = lax.rem(flat + 1, E * N)
    preceding = lax.rem(flat + E * N - 1, E * N)

    def peer(k):
        return {"expert": xor(me, k, E)}

    def at_flat(f):
        return {"expert": lax.div(f, N), "narrow": lax.rem(f, N)}

    barrier = pltpu.get_barrier_semaphore()
    for k in range(1, E):
        pl.semaphore_signal(barrier, inc=1, device_id=peer(k))
    for j in range(1, N):
        pl.semaphore_signal(barrier, inc=1, device_id={"narrow": lax.rem(z + j, N)})
    pl.semaphore_signal(barrier, inc=1, device_id=at_flat(following))
    pl.semaphore_signal(barrier, inc=1, device_id=at_flat(preceding))

    def chunk(ref, k):
        return ref.at[pl.ds(pl.multiple_of(k * cap, cap), cap)]

    def exchange(which, src, dst, k):
        return pltpu.make_async_remote_copy(
            src_ref=src, dst_ref=dst, send_sem=sems.at[which, 0, k],
            recv_sem=sems.at[which, 1, k], device_id=peer(k))

    def copy_a(k):
        return exchange(0, chunk(send_a, k), chunk(recv_a, k), k)

    def copy_b(k):
        return exchange(1, chunk(send_b, k), chunk(recv_b, k), k)

    def copy_o(k):
        return exchange(2, chunk(send_a, k), chunk(recv_o, k), k)

    def copy_f(k):
        return exchange(3, chunk(send_b, k), chunk(recv_f, k), k)

    def copy_i(k):
        return exchange(4, send_i.at[lax.div(k, per)], recv_i.at[k], k)

    def copy_w(k):
        return exchange(5, send_w.at[k], recv_w.at[k], k)

    def each_peer(g, act):
        for i in range(per):
            k = g * per + i

            @pl.when(k != 0)
            def _():
                act(k)

    def line(way, shard):
        return pltpu.make_async_remote_copy(
            src_ref=shards.at[shard], dst_ref=shards.at[shard],
            send_sem=zsems.at[way, 0, shard], recv_sem=zsems.at[way, 1, shard],
            device_id={"narrow": z + 1 - 2 * way})

    def relay(step, begin):
        up, down = z - step, z + step

        @pl.when((up >= 0) & (z + 1 < N))
        def _():
            begin(line(0, up))

        @pl.when((down < N) & (z > 0))
        def _():
            begin(line(1, down))

    number = lax.broadcasted_iota(jnp.int32, (E, rows), 0)
    partner = jnp.bitwise_xor(tgt_row[...], me)
    named = jnp.where(jnp.broadcast_to(partner, (E, rows)) == number, 1.0, 0.0)
    upper = jnp.where(
        lax.broadcasted_iota(jnp.int32, (rows, rows), 0)
        <= lax.broadcasted_iota(jnp.int32, (rows, rows), 1), 1.0, 0.0).astype(BF16)
    count = mm(named.astype(BF16), upper)
    slot = jnp.sum(named * count, axis=0, keepdims=True) - 1.0
    place = (partner * cap).astype(F32) + slot
    offset = ids_row[...] - flat * IMG_DEV
    offset = jnp.where(offset < 0, offset + IMAGES, offset) + 1
    offset8 = jnp.broadcast_to(offset.astype(F32), (8, rows)).astype(BF16)

    tail = prows // 16 * 16
    shards[z, tail:, :] = jnp.zeros((padded - tail, width), BF16)
    shards[z, :prows, :] = params[0]

    pl.semaphore_wait(barrier, E - 1 + N - 1 + 2)
    relay(0, lambda copy: copy.start())

    def pack_feats(i, carry):
        g = groups - 1 - i
        span = pl.ds(pl.multiple_of(g * GROUP, GROUP), GROUP)
        wanted = (lax.broadcasted_iota(jnp.int32, (GROUP, rows), 0) + g * GROUP).astype(F32)
        chosen = jnp.where(jnp.broadcast_to(place, (GROUP, rows)) == wanted, 1.0, 0.0).astype(BF16)
        pick[span, :] = chosen
        send_a[span, :] = mm(chosen, feats[...]).astype(BF16)
        send_i[g] = mm_nt(offset8, chosen)
        each_peer(g, lambda k: (copy_a(k).start(), copy_i(k).start()))
        return carry

    lax.fori_loop(0, groups, pack_feats, 0)
    recv_a[:cap, :] = send_a[:cap, :]
    recv_i[0] = send_i[0]

    def pass_shards(step):
        @pl.when(z - step >= 0)
        def _():
            line(0, z - step).wait_recv()

        @pl.when(z + step < N)
        def _():
            line(1, z + step).wait_recv()

        if step < N - 1:
            relay(step, lambda copy: copy.start())

    pass_shards(1)

    def pack_cot(i, carry):
        g = groups - 1 - i
        span = pl.ds(pl.multiple_of(g * GROUP, GROUP), GROUP)
        send_b[span, :] = mm(pick[span, :], cot[...]).astype(BF16)
        each_peer(g, lambda k: copy_b(k).start())
        return carry

    lax.fori_loop(0, groups, pack_cot, 0)
    recv_b[:cap, :] = send_b[:cap, :]

    turned = jnp.transpose(codes_t[...].astype(F32))
    codes[...] = jnp.zeros_like(codes)
    codes[:IMAGES, : turned.shape[1]] = turned
    codes[IMAGES:, : turned.shape[1]] = turned[:IMG_DEV]

    place_col[...] = jnp.transpose(jnp.broadcast_to(place, (LANES, rows)))

    def unpick_tile(i, carry):
        span = pl.ds(pl.multiple_of(i * GROUP, GROUP), GROUP)
        where = place_col[span, :][:, 0:1]
        for h in range(2):
            index = (lax.broadcasted_iota(jnp.int32, (GROUP, rows), 1) + h * rows).astype(F32)
            pick[pl.ds(pl.multiple_of(h * rows + i * GROUP, GROUP), GROUP), :] = jnp.where(
                jnp.broadcast_to(where, (GROUP, rows)) == index, 1.0, 0.0).astype(BF16)
        return carry

    lax.fori_loop(0, rows // GROUP, unpick_tile, 0)
    for step in range(2, N):
        pass_shards(step)

    for n in range(N):
        wide[n * prows : (n + 1) * prows, :] = shards[n].astype(F32)[:prows]
    weights[...] = wide[:depth, :].astype(BF16)
    code_w[...] = jnp.zeros_like(code_w)
    code_w[:extra, :] = wide[depth : N * prows, :].astype(BF16)

    def picked_images(g, i):
        held = recv_i[g * per + i][0:1, :]
        image = (lax.broadcasted_iota(jnp.int32, (16, GROUP), 0) + 1).astype(F32)
        hit = jnp.broadcast_to(held, (16, GROUP)) == image
        if per > 1:
            inside = lax.div(lax.broadcasted_iota(jnp.int32, (16, GROUP), 1), cap) == i
            hit = hit & inside
        return jnp.where(hit, 1.0, 0.0).astype(BF16)

    def both(t):
        pair = [groups - 1 - 2 * t, groups - 2 - 2 * t]
        return [(g, pl.ds(pl.multiple_of(g * GROUP, GROUP), GROUP)) for g in pair]

    def onward(t, carry):
        for g, span in both(t):
            each_peer(g, lambda k: (copy_a(k).wait_recv(), copy_i(k).wait_recv(), copy_a(k).wait_send()))
        current = []
        for g, span in both(t):
            looked = jnp.zeros((GROUP, LANES), F32)
            for i in range(per):
                source = xor(me, g * per + i, E) * N + z
                first = pl.multiple_of(source * IMG_DEV, IMG_DEV)
                looked = looked + mm_tn(picked_images(g, i), codes[pl.ds(first, 16), :].astype(BF16))
            code_rows[span, :] = looked.astype(BF16)
            current.append(recv_a[span, :])
        for l in range(LAYERS):
            pres = []
            for h, (g, span) in enumerate(both(t)):
                pre = mm(current[h], weights[l * width : (l + 1) * width, :])
                if l == 0:
                    pre = pre + mm(code_rows[span, :], code_w[...])
                pres.append(pre)
            for h, (g, span) in enumerate(both(t)):
                pre = pres[h]
                s = 1.0 / (1.0 + jnp.exp(-pre))
                z_l = (pre * s).astype(BF16)
                slopes[l, span, :] = (s * (1.0 + pre * (1.0 - s))).astype(BF16)
                if l < LAYERS - 1:
                    acts[l, span, :] = z_l
                else:
                    send_a[span, :] = z_l
                current[h] = z_l
        for g, span in both(t):
            each_peer(g, lambda k: copy_o(k).start())
        return carry

    lax.fori_loop(0, groups // 2, onward, 0)
    recv_o[:cap, :] = send_a[:cap, :]

    wide[...] = jnp.zeros_like(wide)

    def copy_d(dest, source):
        return pltpu.make_async_remote_copy(
            src_ref=send_d.at[dest], dst_ref=recv_d.at[source], send_sem=zsems.at[2, 0, dest],
            recv_sem=zsems.at[2, 1, source], device_id={"narrow": dest})

    def copy_c(source):
        return pltpu.make_async_remote_copy(
            src_ref=send_c, dst_ref=recv_c.at[source], send_sem=zsems.at[3, 0, 0],
            recv_sem=zsems.at[3, 1, source], device_id={"narrow": N - 1})

    for l in range(LAYERS - 1, -1, -1):
        rows_l = slice(l * width, (l + 1) * width)

        def back(t, carry, l=l, rows_l=rows_l):
            if l == LAYERS - 1:
                for g, span in both(t):
                    each_peer(g, lambda k: (copy_b(k).wait_recv(), copy_b(k).wait_send()))
            for g, span in both(t):
                up = recv_b[span, :].astype(F32) if l == LAYERS - 1 else ups[span, :]
                err = (up * slopes[l, span, :].astype(F32)).astype(BF16)
                slopes[l, span, :] = err
                if l > 0:
                    ups[span, :] = mm_nt(err, weights[rows_l, :])
            whole = pl.ds(pl.multiple_of((groups - 2 - 2 * t) * GROUP, 2 * GROUP), 2 * GROUP)
            values = recv_a[whole, :] if l == 0 else acts[l - 1, whole, :]
            wide[rows_l, :] += mm_tn(values, slopes[l, whole, :])
            if l == 0:
                wide[depth:, :] += mm_tn(code_rows[whole, :], slopes[l, whole, :])
            return carry

        lax.fori_loop(0, groups // 2, back, 0)
        if l == 0:
            send_c[...] = wide[depth : depth + extra, :].astype(BF16)

            @pl.when(z != N - 1)
            def _():
                copy_c(z).start()

        for n in range(N - 1, -1, -1):
            if n * prows // width == l:
                send_d[n] = wide[n * prows : n * prows + padded, :].astype(BF16)
                if n == N - 1:
                    start = depth - n * prows
                    send_d[n, start:, :] = jnp.zeros((padded - start, width), BF16)

                @pl.when(z != n)
                def _(n=n):
                    copy_d(n, z).start()

    def last(t, carry):
        for g, span in both(t):
            err = slopes[0, span, :]
            send_b[span, :] = mm_nt(err, weights[:width, :]).astype(BF16)
            code_back = mm_nt(err, code_w[...]).astype(BF16)
            for i in range(per):
                send_w[g * per + i] = mm(picked_images(g, i), code_back)
        for g, span in both(t):
            each_peer(g, lambda k: (copy_f(k).start(), copy_w(k).start()))
        return carry

    lax.fori_loop(0, groups // 2, last, 0)
    recv_f[:cap, :] = send_b[:cap, :]
    recv_w[0] = send_w[0]

    each = recv_w[0]
    for k in range(1, E):
        copy_w(k).wait_recv()
        each = each + recv_w[k]
    half[...] = each[IMG_DEV:]
    pass_on = pltpu.make_async_remote_copy(
        src_ref=half, dst_ref=half_in, send_sem=nsems.at[0], recv_sem=nsems.at[1],
        device_id=at_flat(following))
    pass_on.start()

    for copy, held, result in ((copy_o, recv_o, out_rows), (copy_f, recv_f, feat_grad)):
        for k in range(E // 2, E):
            copy(k).wait_recv()

        def upper_half(i, carry, held=held):
            span = pl.ds(pl.multiple_of(i * GROUP, GROUP), GROUP)
            second = pl.ds(pl.multiple_of(rows + i * GROUP, GROUP), GROUP)
            ups[span, :] = mm(pick[second, :], held[rows:, :])
            return carry

        lax.fori_loop(0, rows // GROUP, upper_half, 0)
        for k in range(1, E // 2):
            copy(k).wait_recv()

        def lower_half(i, carry, held=held, result=result):
            span = pl.ds(pl.multiple_of(i * GROUP, GROUP), GROUP)
            result[span, :] = (ups[span, :] + mm(pick[span, :], held[:rows, :])).astype(BF16)
            return carry

        lax.fori_loop(0, rows // GROUP, lower_half, 0)

    pass_on.wait()
    code_grad[...] = each[:IMG_DEV] + half_in[...]

    for j in range(1, N):
        copy_d(0, lax.rem(z + j, N)).wait_recv()
    total = send_d[z].astype(F32)
    for j in range(1, N):
        total = total + recv_d[lax.rem(z + j, N)].astype(F32)
    blocks = width // LANES
    for c in range(blocks):
        param_grad[pl.ds(c, prows, blocks), :] = total[:prows, c * LANES : (c + 1) * LANES]

    @pl.when(z == N - 1)
    def _():
        terms = send_c[...].astype(F32)
        for source in range(N - 1):
            copy_c(source).wait_recv()
            terms = terms + recv_c[source].astype(F32)
        start = (prows - extra) * blocks
        for c in range(blocks):
            param_grad[pl.ds(start + c, extra, blocks), :] = terms[:, c * LANES : (c + 1) * LANES]

    for step in range(N - 1):
        relay(step, lambda copy: copy.wait_send())
    for n in range(N):
        @pl.when(z != n)
        def _(n=n):
            copy_d(n, z).wait_send()

    @pl.when(z != N - 1)
    def _():
        copy_c(z).wait_send()

    for k in range(1, E):
        for copy in (copy_o, copy_f, copy_i, copy_w):
            copy(k).wait_send()


def body(E, N, feats, cotangent, routes, image_ids, codes, params):
    rows, width = feats.shape
    prows = params.shape[1]
    padded = -(-prows // 16) * 16
    images, code = codes.shape
    deep = LAYERS * width + LANES
    extra = N * prows - LAYERS * width
    vm = pl.BlockSpec(memory_space=pltpu.VMEM)
    slots = 2 * rows
    buffer = pltpu.VMEM((slots, width), BF16)
    per = GROUP // (slots // E)
    groups = slots // GROUP
    out_rows, feat_grad, param_grad, code_grad = pl.pallas_call(
        functools.partial(kernel, E, N, images),
        out_shape=[
            jax.ShapeDtypeStruct((rows, width), BF16),
            jax.ShapeDtypeStruct((rows, width), BF16),
            jax.ShapeDtypeStruct((prows * width // LANES, LANES), F32),
            jax.ShapeDtypeStruct((IMG_DEV, LANES), F32),
        ],
        in_specs=[vm] * 6,
        out_specs=[vm] * 4,
        scratch_shapes=[
            buffer, buffer,
            pltpu.VMEM((groups, 8, GROUP), F32),
            pltpu.VMEM((E, 16, LANES), F32),
            pltpu.VMEM((N, padded, width), BF16),
            buffer, buffer,
            pltpu.VMEM((E, 8, GROUP), F32),
            pltpu.VMEM((E, 16, LANES), F32),
            pltpu.VMEM((N, padded, width), BF16),
            buffer, buffer,
            pltpu.VMEM((N, padded, width), BF16),
            pltpu.VMEM((deep, width), F32),
            pltpu.VMEM((LAYERS * width, width), BF16),
            pltpu.VMEM((LANES, width), BF16),
            pltpu.VMEM((LAYERS - 1, slots, width), BF16),
            pltpu.VMEM((LAYERS, slots, width), BF16),
            pltpu.VMEM((slots, LANES), BF16),
            pltpu.VMEM((slots, rows), BF16),
            pltpu.VMEM((rows, LANES), F32),
            pltpu.VMEM((slots, width), F32),
            pltpu.VMEM((images + IMG_DEV, LANES), F32),
            pltpu.VMEM((extra, width), BF16),
            pltpu.VMEM((N, extra, width), BF16),
            pltpu.VMEM((IMG_DEV, LANES), F32),
            pltpu.VMEM((IMG_DEV, LANES), F32),
            pltpu.SemaphoreType.DMA((6, 2, E)),
            pltpu.SemaphoreType.DMA((4, 2, N)),
            pltpu.SemaphoreType.DMA((2,)),
        ],
        compiler_params=pltpu.CompilerParams(
            collective_id=0, has_side_effects=True, vmem_limit_bytes=60 * 1024 * 1024),
    )(
        feats, cotangent, routes.reshape(1, rows),
        image_ids.reshape(1, rows), codes.T, params,
    )
    return out_rows, feat_grad, param_grad.reshape(1, prows, width), code_grad[:, :code]


def solution(mesh):
    E, N = mesh.shape["expert"], mesh.shape["narrow"]
    rows = P(("expert", "narrow"), None)
    held = P("expert", "narrow", None)
    return jax.shard_map(
        functools.partial(body, E, N), mesh=mesh,
        in_specs=(rows, rows, rows, P(("expert", "narrow")), P(), held),
        out_specs=(rows, rows, held, rows), check_vma=False)
```

```python
import functools

import jax
import jax.numpy as jnp
from jax import lax
from jax.experimental import pallas as pl
from jax.experimental.pallas import tpu as pltpu
from jax.sharding import PartitionSpec as P

LAYERS = 4
IMG_DEV = 8
GROUP = 256
LANES = 128
F32 = jnp.float32
BF16 = jnp.bfloat16


def xor(a, b, extent):
    total, bit = 0, 1
    while bit < extent:
        x = lax.rem(lax.div(a, bit), 2)
        y = lax.rem(lax.div(b, bit), 2)
        total = total + bit * (x + y - 2 * x * y)
        bit *= 2
    return total


def mm(a, b):
    return jnp.dot(a, b, preferred_element_type=F32)


def mm_nt(a, b):
    return lax.dot_general(a, b, (((1,), (1,)), ((), ())), preferred_element_type=F32)


def mm_tn(a, b):
    return lax.dot_general(a, b, (((0,), (0,)), ((), ())), preferred_element_type=F32)


def kernel(
    E, N, IMAGES, feats, cot, tgt_row, ids_row, codes_t, params,
    out_rows, feat_grad, param_grad, code_grad,
    send_a, send_b, send_i, send_w, send_d,
    recv_a, recv_b, recv_i, recv_w, recv_d, recv_o, recv_f,
    shards, wide, weights, code_w, acts, slopes, code_rows, pick, place_col,
    ups, codes, send_c, recv_c, half, half_in, sems, zsems, nsems,
):
    rows, width = feats.shape
    prows = params.shape[1]
    cap = 2 * rows // E
    per = GROUP // cap
    groups = 2 * rows // GROUP
    padded = shards.shape[1]
    depth = LAYERS * width
    extra = N * prows - depth
    me = lax.axis_index("expert")
    z = lax.axis_index("narrow")
    flat = me * N + z
    following = lax.rem(flat + 1, E * N)
    preceding = lax.rem(flat + E * N - 1, E * N)

    def peer(k):
        return {"expert": xor(me, k, E)}

    def at_flat(f):
        return {"expert": lax.div(f, N), "narrow": lax.rem(f, N)}

    barrier = pltpu.get_barrier_semaphore()
    for k in range(1, E):
        pl.semaphore_signal(barrier, inc=1, device_id=peer(k))
    for j in range(1, N):
        pl.semaphore_signal(barrier, inc=1, device_id={"narrow": lax.rem(z + j, N)})
    pl.semaphore_signal(barrier, inc=1, device_id=at_flat(following))
    pl.semaphore_signal(barrier, inc=1, device_id=at_flat(preceding))

    def chunk(ref, k):
        return ref.at[pl.ds(pl.multiple_of(k * cap, cap), cap)]

    def exchange(which, src, dst, k):
        return pltpu.make_async_remote_copy(
            src_ref=src, dst_ref=dst, send_sem=sems.at[which, 0, k],
            recv_sem=sems.at[which, 1, k], device_id=peer(k))

    def copy_a(k):
        return exchange(0, chunk(send_a, k), chunk(recv_a, k), k)

    def copy_b(k):
        return exchange(1, chunk(send_b, k), chunk(recv_b, k), k)

    def copy_o(k):
        return exchange(2, chunk(send_a, k), chunk(recv_o, k), k)

    def copy_f(k):
        return exchange(3, chunk(send_b, k), chunk(recv_f, k), k)

    def copy_i(k):
        return exchange(4, send_i.at[lax.div(k, per)], recv_i.at[k], k)

    def copy_w(k):
        return exchange(5, send_w.at[k], recv_w.at[k], k)

    def each_peer(g, act):
        for i in range(per):
            k = g * per + i

            @pl.when(k != 0)
            def _():
                act(k)

    def line(way, shard):
        return pltpu.make_async_remote_copy(
            src_ref=shards.at[shard], dst_ref=shards.at[shard],
            send_sem=zsems.at[way, 0, shard], recv_sem=zsems.at[way, 1, shard],
            device_id={"narrow": z + 1 - 2 * way})

    def relay(step, begin):
        up, down = z - step, z + step

        @pl.when((up >= 0) & (z + 1 < N))
        def _():
            begin(line(0, up))

        @pl.when((down < N) & (z > 0))
        def _():
            begin(line(1, down))

    number = lax.broadcasted_iota(jnp.int32, (E, rows), 0)
    partner = jnp.bitwise_xor(tgt_row[...], me)
    named = jnp.where(jnp.broadcast_to(partner, (E, rows)) == number, 1.0, 0.0)
    upper = jnp.where(
        lax.broadcasted_iota(jnp.int32, (rows, rows), 0)
        <= lax.broadcasted_iota(jnp.int32, (rows, rows), 1), 1.0, 0.0).astype(BF16)
    count = mm(named.astype(BF16), upper)
    slot = jnp.sum(named * count, axis=0, keepdims=True) - 1.0
    place = (partner * cap).astype(F32) + slot
    offset = ids_row[...] - flat * IMG_DEV
    offset = jnp.where(offset < 0, offset + IMAGES, offset) + 1
    offset8 = jnp.broadcast_to(offset.astype(F32), (8, rows)).astype(BF16)

    tail = prows // 16 * 16
    shards[z, tail:, :] = jnp.zeros((padded - tail, width), BF16)
    shards[z, :prows, :] = params[0]

    pl.semaphore_wait(barrier, E - 1 + N - 1 + 2)
    relay(0, lambda copy: copy.start())

    def pack_feats(i, carry):
        g = groups - 1 - i
        span = pl.ds(pl.multiple_of(g * GROUP, GROUP), GROUP)
        wanted = (lax.broadcasted_iota(jnp.int32, (GROUP, rows), 0) + g * GROUP).astype(F32)
        chosen = jnp.where(jnp.broadcast_to(place, (GROUP, rows)) == wanted, 1.0, 0.0).astype(BF16)
        pick[span, :] = chosen
        send_a[span, :] = mm(chosen, feats[...]).astype(BF16)
        send_i[g] = mm_nt(offset8, chosen)
        each_peer(g, lambda k: (copy_a(k).start(), copy_i(k).start()))
        return carry

    lax.fori_loop(0, groups, pack_feats, 0)
    recv_a[:cap, :] = send_a[:cap, :]
    recv_i[0] = send_i[0]

    def pass_shards(step):
        @pl.when(z - step >= 0)
        def _():
            line(0, z - step).wait_recv()

        @pl.when(z + step < N)
        def _():
            line(1, z + step).wait_recv()

        if step < N - 1:
            relay(step, lambda copy: copy.start())

    def widen(step):
        for n in range(N):
            @pl.when((z == n + step) | (z == n - step))
            def _(n=n):
                wide[n * prows : (n + 1) * prows, :] = shards[n].astype(F32)[:prows]

    pass_shards(1)

    def pack_cot(i, carry):
        g = groups - 1 - i
        span = pl.ds(pl.multiple_of(g * GROUP, GROUP), GROUP)
        send_b[span, :] = mm(pick[span, :], cot[...]).astype(BF16)
        each_peer(g, lambda k: copy_b(k).start())
        return carry

    lax.fori_loop(0, groups, pack_cot, 0)
    recv_b[:cap, :] = send_b[:cap, :]

    turned = jnp.transpose(codes_t[...].astype(F32))
    codes[...] = jnp.zeros_like(codes)
    codes[:IMAGES, : turned.shape[1]] = turned
    codes[IMAGES:, : turned.shape[1]] = turned[:IMG_DEV]

    place_col[...] = jnp.transpose(jnp.broadcast_to(place, (LANES, rows)))

    def unpick_tile(i, carry):
        span = pl.ds(pl.multiple_of(i * GROUP, GROUP), GROUP)
        where = place_col[span, :][:, 0:1]
        for h in range(2):
            index = (lax.broadcasted_iota(jnp.int32, (GROUP, rows), 1) + h * rows).astype(F32)
            pick[pl.ds(pl.multiple_of(h * rows + i * GROUP, GROUP), GROUP), :] = jnp.where(
                jnp.broadcast_to(where, (GROUP, rows)) == index, 1.0, 0.0).astype(BF16)
        return carry

    lax.fori_loop(0, rows // GROUP, unpick_tile, 0)
    widen(0)
    widen(1)
    for step in range(2, N):
        pass_shards(step)
        widen(step)

    weights[...] = wide[:depth, :].astype(BF16)
    code_w[...] = jnp.zeros_like(code_w)
    code_w[:extra, :] = wide[depth : N * prows, :].astype(BF16)

    def picked_images(g, i):
        held = recv_i[g * per + i][0:1, :]
        image = (lax.broadcasted_iota(jnp.int32, (16, GROUP), 0) + 1).astype(F32)
        hit = jnp.broadcast_to(held, (16, GROUP)) == image
        if per > 1:
            inside = lax.div(lax.broadcasted_iota(jnp.int32, (16, GROUP), 1), cap) == i
            hit = hit & inside
        return jnp.where(hit, 1.0, 0.0).astype(BF16)

    BLOCK = 2 * GROUP
    steps = groups // 4

    def four(t):
        return [groups - 1 - 4 * t - i for i in range(4)]

    def span_of(g, extent):
        return pl.ds(pl.multiple_of(g * GROUP, extent), extent)

    def halves(t):
        return [span_of(groups - 2 - 4 * t, BLOCK), span_of(groups - 4 - 4 * t, BLOCK)]

    def onward(t, carry):
        for g in four(t):
            each_peer(g, lambda k: (copy_a(k).wait_recv(), copy_i(k).wait_recv(), copy_a(k).wait_send()))
        for g in four(t):
            looked = jnp.zeros((GROUP, LANES), F32)
            for i in range(per):
                source = xor(me, g * per + i, E) * N + z
                first = pl.multiple_of(source * IMG_DEV, IMG_DEV)
                looked = looked + mm_tn(picked_images(g, i), codes[pl.ds(first, 16), :].astype(BF16))
            code_rows[span_of(g, GROUP), :] = looked.astype(BF16)
        for l in range(LAYERS):
            pres = []
            for span in halves(t):
                current = recv_a[span, :] if l == 0 else acts[l - 1, span, :]
                pre = mm(current, weights[l * width : (l + 1) * width, :])
                if l == 0:
                    pre = pre + mm(code_rows[span, :], code_w[...])
                pres.append(pre)
            for pre, span in zip(pres, halves(t)):
                s = 0.5 + 0.5 * jnp.tanh(0.5 * pre)
                z_l = pre * s
                slopes[l, span, :] = (s + z_l * (1.0 - s)).astype(BF16)
                if l < LAYERS - 1:
                    acts[l, span, :] = z_l.astype(BF16)
                else:
                    send_a[span, :] = z_l.astype(BF16)
        for g in four(t):
            each_peer(g, lambda k: copy_o(k).start())
        return carry

    lax.fori_loop(0, steps, onward, 0)
    recv_o[:cap, :] = send_a[:cap, :]

    wide[...] = jnp.zeros_like(wide)

    def copy_d(dest, source):
        return pltpu.make_async_remote_copy(
            src_ref=send_d.at[dest], dst_ref=recv_d.at[source], send_sem=zsems.at[2, 0, dest],
            recv_sem=zsems.at[2, 1, source], device_id={"narrow": dest})

    def copy_c(source):
        return pltpu.make_async_remote_copy(
            src_ref=send_c, dst_ref=recv_c.at[source], send_sem=zsems.at[3, 0, 0],
            recv_sem=zsems.at[3, 1, source], device_id={"narrow": N - 1})

    for l in range(LAYERS - 1, -1, -1):
        rows_l = slice(l * width, (l + 1) * width)

        def back(t, carry, l=l, rows_l=rows_l):
            if l == LAYERS - 1:
                for g in four(t):
                    each_peer(g, lambda k: (copy_b(k).wait_recv(), copy_b(k).wait_send()))
            for span in halves(t):
                up = recv_b[span, :].astype(F32) if l == LAYERS - 1 else ups[span, :]
                err = (up * slopes[l, span, :].astype(F32)).astype(BF16)
                slopes[l, span, :] = err
                if l > 0:
                    ups[span, :] = mm_nt(err, weights[rows_l, :])
            whole = span_of(groups - 4 - 4 * t, 4 * GROUP)
            values = recv_a[whole, :] if l == 0 else acts[l - 1, whole, :]
            wide[rows_l, :] += mm_tn(values, slopes[l, whole, :])
            if l == 0:
                wide[depth:, :] += mm_tn(code_rows[whole, :], slopes[l, whole, :])
            return carry

        lax.fori_loop(0, steps, back, 0)
        if l == 0:
            send_c[...] = wide[depth : depth + extra, :].astype(BF16)

            @pl.when(z != N - 1)
            def _():
                copy_c(z).start()

        for n in range(N - 1, -1, -1):
            if n * prows // width == l:
                send_d[n] = wide[n * prows : n * prows + padded, :].astype(BF16)
                if n == N - 1:
                    start = depth - n * prows
                    send_d[n, start:, :] = jnp.zeros((padded - start, width), BF16)

                @pl.when(z != n)
                def _(n=n):
                    copy_d(n, z).start()

    def last(t, carry):
        for g in (groups - 1 - 2 * t, groups - 2 - 2 * t):
            span = span_of(g, GROUP)
            err = slopes[0, span, :]
            send_b[span, :] = mm_nt(err, weights[:width, :]).astype(BF16)
            code_back = mm_nt(err, code_w[...]).astype(BF16)
            for i in range(per):
                send_w[g * per + i] = mm(picked_images(g, i), code_back)
        for g in (groups - 1 - 2 * t, groups - 2 - 2 * t):
            each_peer(g, lambda k: (copy_f(k).start(), copy_w(k).start()))
        return carry

    lax.fori_loop(0, groups // 2, last, 0)
    recv_f[:cap, :] = send_b[:cap, :]
    recv_w[0] = send_w[0]

    each = recv_w[0]
    for k in range(1, E):
        copy_w(k).wait_recv()
        each = each + recv_w[k]
    half[...] = each[IMG_DEV:]
    pass_on = pltpu.make_async_remote_copy(
        src_ref=half, dst_ref=half_in, send_sem=nsems.at[0], recv_sem=nsems.at[1],
        device_id=at_flat(following))
    pass_on.start()

    for copy, held, result in ((copy_o, recv_o, out_rows), (copy_f, recv_f, feat_grad)):
        for k in range(E // 2, E):
            copy(k).wait_recv()

        def upper_half(i, carry, held=held):
            span = pl.ds(pl.multiple_of(i * GROUP, GROUP), GROUP)
            second = pl.ds(pl.multiple_of(rows + i * GROUP, GROUP), GROUP)
            ups[span, :] = mm(pick[second, :], held[rows:, :])
            return carry

        lax.fori_loop(0, rows // GROUP, upper_half, 0)
        for k in range(1, E // 2):
            copy(k).wait_recv()

        def lower_half(i, carry, held=held, result=result):
            span = pl.ds(pl.multiple_of(i * GROUP, GROUP), GROUP)
            result[span, :] = (ups[span, :] + mm(pick[span, :], held[:rows, :])).astype(BF16)
            return carry

        lax.fori_loop(0, rows // GROUP, lower_half, 0)

    pass_on.wait()
    code_grad[...] = each[:IMG_DEV] + half_in[...]

    for j in range(1, N):
        copy_d(0, lax.rem(z + j, N)).wait_recv()
    total = send_d[z].astype(F32)
    for j in range(1, N):
        total = total + recv_d[lax.rem(z + j, N)].astype(F32)
    blocks = width // LANES
    for c in range(blocks):
        param_grad[pl.ds(c, prows, blocks), :] = total[:prows, c * LANES : (c + 1) * LANES]

    @pl.when(z == N - 1)
    def _():
        terms = send_c[...].astype(F32)
        for source in range(N - 1):
            copy_c(source).wait_recv()
            terms = terms + recv_c[source].astype(F32)
        start = (prows - extra) * blocks
        for c in range(blocks):
            param_grad[pl.ds(start + c, extra, blocks), :] = terms[:, c * LANES : (c + 1) * LANES]

    for step in range(N - 1):
        relay(step, lambda copy: copy.wait_send())
    for n in range(N):
        @pl.when(z != n)
        def _(n=n):
            copy_d(n, z).wait_send()

    @pl.when(z != N - 1)
    def _():
        copy_c(z).wait_send()

    for k in range(1, E):
        for copy in (copy_o, copy_f, copy_i, copy_w):
            copy(k).wait_send()


def body(E, N, feats, cotangent, routes, image_ids, codes, params):
    rows, width = feats.shape
    prows = params.shape[1]
    padded = -(-prows // 16) * 16
    images, code = codes.shape
    deep = LAYERS * width + LANES
    extra = N * prows - LAYERS * width
    vm = pl.BlockSpec(memory_space=pltpu.VMEM)
    slots = 2 * rows
    buffer = pltpu.VMEM((slots, width), BF16)
    per = GROUP // (slots // E)
    groups = slots // GROUP
    out_rows, feat_grad, param_grad, code_grad = pl.pallas_call(
        functools.partial(kernel, E, N, images),
        out_shape=[
            jax.ShapeDtypeStruct((rows, width), BF16),
            jax.ShapeDtypeStruct((rows, width), BF16),
            jax.ShapeDtypeStruct((prows * width // LANES, LANES), F32),
            jax.ShapeDtypeStruct((IMG_DEV, LANES), F32),
        ],
        in_specs=[vm] * 6,
        out_specs=[vm] * 4,
        scratch_shapes=[
            buffer, buffer,
            pltpu.VMEM((groups, 8, GROUP), F32),
            pltpu.VMEM((E, 16, LANES), F32),
            pltpu.VMEM((N, padded, width), BF16),
            buffer, buffer,
            pltpu.VMEM((E, 8, GROUP), F32),
            pltpu.VMEM((E, 16, LANES), F32),
            pltpu.VMEM((N, padded, width), BF16),
            buffer, buffer,
            pltpu.VMEM((N, padded, width), BF16),
            pltpu.VMEM((deep, width), F32),
            pltpu.VMEM((LAYERS * width, width), BF16),
            pltpu.VMEM((LANES, width), BF16),
            pltpu.VMEM((LAYERS - 1, slots, width), BF16),
            pltpu.VMEM((LAYERS, slots, width), BF16),
            pltpu.VMEM((slots, LANES), BF16),
            pltpu.VMEM((slots, rows), BF16),
            pltpu.VMEM((rows, LANES), F32),
            pltpu.VMEM((slots, width), F32),
            pltpu.VMEM((images + IMG_DEV, LANES), F32),
            pltpu.VMEM((extra, width), BF16),
            pltpu.VMEM((N, extra, width), BF16),
            pltpu.VMEM((IMG_DEV, LANES), F32),
            pltpu.VMEM((IMG_DEV, LANES), F32),
            pltpu.SemaphoreType.DMA((6, 2, E)),
            pltpu.SemaphoreType.DMA((4, 2, N)),
            pltpu.SemaphoreType.DMA((2,)),
        ],
        compiler_params=pltpu.CompilerParams(
            collective_id=0, has_side_effects=True, vmem_limit_bytes=60 * 1024 * 1024),
    )(
        feats, cotangent, routes.reshape(1, rows),
        image_ids.reshape(1, rows), codes.T, params,
    )
    return out_rows, feat_grad, param_grad.reshape(1, prows, width), code_grad[:, :code]


def solution(mesh):
    E, N = mesh.shape["expert"], mesh.shape["narrow"]
    rows = P(("expert", "narrow"), None)
    held = P("expert", "narrow", None)
    return jax.shard_map(
        functools.partial(body, E, N), mesh=mesh,
        in_specs=(rows, rows, rows, P(("expert", "narrow")), P(), held),
        out_specs=(rows, rows, held, rows), check_vma=False)
```
